256 devices in a mesh: dp: 8 (over z), expert: 32 (over x, y, core).
Axes of the slice: x: 4, y: 4, z: 8, core: 2. Of those that a mesh axis runs over, the one named last changes fastest.
Arguments:
- tokens: bfloat16 [32768, 2048], P(('dp', 'expert')), parts along dimension 0, may hold values from -6 to 6
- routes: int32 [32768, 8], P(('dp', 'expert')), parts along dimension 0, may hold values from 0 to 31, all different within a row; in each aligned block of 128 rows (0 to 127, 128 to 255, ...) at most 40 rows name the same one
- gate_num: int32 [32768, 8], P(('dp', 'expert')), parts along dimension 0, may hold values from 1 to 1023
- w_gate: bfloat16 [32, 2048, 768], P('expert'), may hold values from -0.125 to 0.125
- w_up: bfloat16 [32, 2048, 768], P('expert'), may hold values from -0.125 to 0.125
- w_down: bfloat16 [32, 768, 2048], P('expert'), may hold values from -0.21875 to 0.21875
Outputs:
- combined: bfloat16 [32768, 2048], P(('dp', 'expert')), parts along dimension 0
The draws below stay inside these ranges and needn't reach their ends.
There are 8 independent parts, one for each index of `dp`. The reference program is written for one: setup_inputs(seed, part) draws one part's arguments, and reference() takes and returns one part's arrays. A program takes and returns all parts, laid end to end along the dimension named above; an argument that names none is the same for every part. Nothing has to cross between parts.
Inputs may be any that keep to these rules, and one draw needn't show every extreme that they name: `routes`: each row names 8 different experts; among the rows of one device no expert is named more than 40 times, a bound that some block reaches.
All inputs are finite; a program needn't handle non-finite values.
Results may differ from the reference program's by a relative error of at most 0.0057.
Values may be sent and summed in bfloat16 or wider, within the bound.
No kernel may reach another device: no remote copies, remote signals or barrier semaphores. Data moves between devices by JAX's collectives and lax.ppermute only.
A program may use at most 128 MiB of HBM per device.

```python
import math
import jax
import jax.numpy as jnp
import numpy as np
from jax import lax

D = 2048
HID = 768
TOPK = 8
GATE_DEN = 1024
TOK_DEV = 128
EXPERTS = 32
TOKENS = 4096
CAP = 40
N_EXPERT = 32


def place_ends(values, rng, smallest, high):
    shape = values.shape
    spot = [jax.random.randint(jax.random.fold_in(rng, axis), (), 0, shape[axis]) for axis in range(len(shape))]
    values = values.at[tuple(spot)].set(smallest)
    longest = shape.index(max(shape))
    spot[longest] = (spot[longest] + 1) % shape[longest]
    return values.at[tuple(spot)].set(high)


def level_of(rng, extent, split, low, high):
    gain = 1.0
    for position, blocks in split:
        draws = jax.random.uniform(jax.random.fold_in(jax.random.fold_in(rng, 6), position), (blocks,), jnp.float32, low / len(split), high / len(split))
        gain = gain * jnp.repeat(jnp.exp(draws), extent[position] // blocks).reshape((-1,) + (1,) * (len(extent) - 1 - position))
    return gain


def shared_out(stream_key, own, number, rows, amount, top, bound, slope):
    order = jax.random.permutation(stream_key, amount)
    packed, usual = shares(amount, rows * top, bound, slope, True), shares(amount, rows * top, bound, slope, False)
    places = jnp.arange(amount)

    def named(sizes, turn):
        used = int((sizes > 0).sum())
        fixed = max(1, used // 4)
        passed = fixed + (places - fixed + turn * (used - fixed)) % max(1, amount - fixed)
        return jnp.zeros((amount,), jnp.int32).at[order[jnp.where(places < fixed, places, passed)]].set(jnp.asarray(sizes, jnp.int32))

    sizes = jnp.where(number % 4 == 0, named(packed, number // 4), named(usual, number - number // 4 - 1))
    mixed = jax.random.permutation(jax.random.fold_in(own, 3), amount)
    donor, receiver = mixed[0:amount // 2 * 2:2], mixed[1:amount // 2 * 2:2]
    margin = jnp.minimum(sizes[donor] - 1, bound - sizes[receiver]) // 2
    margin = jnp.where((donor == order[0]) | (receiver == order[0]) | (sizes[receiver] == 0), 0, jnp.maximum(margin, 0))
    passed = jax.random.randint(jax.random.fold_in(own, 4), (amount // 2,), 0, 1 << 20) % (margin + 1)
    sizes = sizes.at[donor].add(-passed).at[receiver].add(passed)
    items = jnp.searchsorted(jnp.cumsum(sizes), jnp.arange(rows * top), side="right").astype(jnp.int32)
    grid = items.reshape(top, rows).T
    grid = grid[jax.random.permutation(jax.random.fold_in(own, 1), rows)]
    turn = jax.random.randint(jax.random.fold_in(own, 2), (rows, 1), 0, top)
    return jnp.take_along_axis(grid, (jnp.arange(top)[None, :] + turn) % top, axis=1)


def shares(count, total, most, lean, full):
    loads = [(1 << 20) // math.isqrt(rank ** lean) + 1 for rank in range(1, count + 1)]
    largest = most if full else min(most, max(-(-total // count), total * loads[0] // sum(loads)))
    least = 1 if total - largest >= count - 1 else 0
    given, spare = [largest] + [least] * (count - 1), total - largest - least * (count - 1)
    while spare > 0:
        movable = [i for i in range(1, count) if given[i] < largest] or [i for i in range(1, count) if given[i] < most]
        pool, left = sum([loads[i] for i in movable]), spare
        for i in movable:
            addition = min(most - given[i], max(1, left * loads[i] // pool), spare)
            given[i] = given[i] + addition
            spare = spare - addition
    return np.array(given)


def normal_values(own_key, shape, deviation, limit, cuts=(), kind=jnp.bfloat16):
    gain = level_of(own_key, shape, cuts, -0.22, 0.18) if cuts else 1.0
    result = jax.random.normal(own_key, shape, jnp.float32) * deviation * gain
    return jnp.minimum(jnp.maximum(result, -limit), limit).astype(kind)


def setup_inputs(seed: int = 0, part: int = 0) -> dict:
    arg_keys = jax.random.split(jax.random.key(seed), 7)
    own_keys = jax.random.split(jax.random.fold_in(arg_keys[6], part), 7)
    tokens = normal_values(own_keys[0], (TOKENS, D), 1.0, 6.0, ((0, 32),))
    routes_keys = jax.random.split(jax.random.fold_in(own_keys[1], 1), TOKENS // TOK_DEV)
    routes_turns = jax.random.permutation(jax.random.fold_in(own_keys[1], 3), TOKENS // TOK_DEV)
    routes = jax.vmap(lambda own, number: shared_out(jax.random.fold_in(own_keys[1], 2), own, number, TOK_DEV, EXPERTS, TOPK, CAP, 2))(routes_keys, routes_turns).reshape((TOKENS, TOPK))
    gate_num = place_ends(jax.random.randint(own_keys[2], (TOKENS, TOPK), 1, GATE_DEN), jax.random.fold_in(own_keys[2], 1), 1, GATE_DEN - 1).astype(jnp.int32)
    w_gate = normal_values(arg_keys[3], (EXPERTS, D, HID), D ** -0.5, 0.125, ((0, 32),))
    w_up = normal_values(arg_keys[4], (EXPERTS, D, HID), D ** -0.5, 0.125, ((0, 32),))
    w_down = normal_values(arg_keys[5], (EXPERTS, HID, D), HID ** -0.5, 0.21875, ((0, 32),))
    return dict(tokens=tokens, routes=routes, gate_num=gate_num, w_gate=w_gate, w_up=w_up, w_down=w_down)


def expert_rows(rows, gate_weight, up_weight, down_weight):
    gate_part = jnp.dot(rows, gate_weight, preferred_element_type=jnp.float32)
    up_part = jnp.dot(rows, up_weight, preferred_element_type=jnp.float32)
    hidden = (jax.nn.silu(gate_part) * up_part).astype(jnp.bfloat16)
    return jnp.dot(hidden, down_weight, preferred_element_type=jnp.float32).astype(jnp.bfloat16)


def reference(tokens, routes, gate_num, w_gate, w_up, w_down):
    weights = gate_num.astype(jnp.float32) / GATE_DEN
    slot_total = N_EXPERT * CAP

    def add_expert(total, expert):
        matches = routes == expert
        weight_sum = jnp.sum(jnp.where(matches, weights, jnp.zeros_like(weights)), axis=1)
        routed = jnp.any(matches, axis=1)
        row_index = jnp.nonzero(routed, size=slot_total, fill_value=0)[0].astype(jnp.int32)
        filled = jnp.arange(slot_total, dtype=jnp.int32) < jnp.sum(routed.astype(jnp.int32))
        outputs = expert_rows(tokens[row_index], w_gate[expert], w_up[expert], w_down[expert])
        factor = jnp.where(filled, weight_sum[row_index], jnp.zeros_like(weight_sum[row_index]))
        weighted = outputs.astype(jnp.float32) * factor[:, None]
        return total.at[row_index].add(weighted), None

    start = jnp.zeros(tokens.shape, jnp.float32)
    total, unused = lax.scan(add_expert, start, jnp.arange(EXPERTS, dtype=jnp.int32))
    return total.astype(jnp.bfloat16)
```

```python
import functools

import jax
import jax.numpy as jnp
from jax import lax
from jax.experimental import pallas as pl
from jax.experimental.pallas import tpu as pltpu
from jax.sharding import Mesh, PartitionSpec as P

GATE_DEN = 1024
META = 128
WIN = 128
BF = jnp.bfloat16
F32 = jnp.float32
RING = 4
NEXT = [(i, (i + 1) % RING) for i in range(RING)]
PREV = [(i, (i + RING - 1) % RING) for i in range(RING)]


def expert_kernel(piece_rows, block, mb, rows_cap, width, ids, *refs):
    n_piece = len(piece_rows)
    pieces, refs = refs[:n_piece], refs[n_piece:]
    weights, refs = refs[:6], refs[6:]
    outs, refs = refs[:n_piece], refs[n_piece:]
    x_s, sel_s, hid_s, y_s, acc_s, out_s, wg_s, wu_s, wd_s, x_sem, w_sem, o_sem = refs
    total = sum(piece_rows)
    n_block = total // block
    hid = wg_s.shape[2]
    starts = [sum(piece_rows[:i]) for i in range(n_piece)]

    x_copies = [
        pltpu.make_async_copy(pieces[i], x_s.at[pl.ds(starts[i], piece_rows[i])], x_sem.at[i])
        for i in range(n_piece)
    ]
    for c in x_copies:
        c.start()
    w_copies = []
    for e in range(2):
        for j, dst in enumerate((wg_s, wu_s, wd_s)):
            c = pltpu.make_async_copy(weights[3 * e + j].at[0], dst.at[e], w_sem.at[3 * e + j])
            c.start()
            w_copies.append(c)

    sel_s[...] = jnp.zeros(sel_s.shape, BF)
    y_s[...] = jnp.zeros(y_s.shape, BF)

    def pick(shape, expert_axis):
        col = lax.broadcasted_iota(jnp.int32, shape, 1 - expert_axis)
        which = lax.broadcasted_iota(jnp.int32, shape, expert_axis)
        mine = jnp.where(which == 0, ids[0], ids[1])
        high = jnp.where(col == mine, 4.0, 0.0)
        low = jnp.where(col == mine + 32, 1.0, 0.0)
        return jnp.where(which < 2, high + low, 0.0).astype(BF)

    pick_row = pick((8, META), 0)
    pick_col = pick((META, META), 1)
    lane = lax.broadcasted_iota(jnp.int32, (block, block), 1)
    sub = lax.broadcasted_iota(jnp.int32, (block, block), 0)
    upper = jnp.where(sub <= lane, 1.0, 0.0).astype(BF)
    lower = jnp.where(lane <= sub, 1.0, 0.0).astype(BF)
    slot_row = lax.broadcasted_iota(jnp.int32, (WIN, block), 0)
    slot_col = lax.broadcasted_iota(jnp.int32, (block, WIN), 1)

    for c in x_copies:
        c.wait()

    base = [jnp.int32(0), jnp.int32(0)]
    first, skew, wins = [], [], []
    for b in range(n_block):
        rows = pl.ds(b * block, block)
        meta = x_s[rows, width:]
        num = lax.dot_general(pick_row, meta, (((1,), (1,)), ((), ())), preferred_element_type=F32)
        hit = jnp.where(num > 0.0, 1.0, 0.0)
        rank = jnp.dot(hit.astype(BF), upper, preferred_element_type=F32)
        place = jnp.where(num > 0.0, rank - 1.0, -1.0e4).astype(jnp.int32)
        start, off, need = [], [], []
        for e in range(2):
            count = jnp.sum(hit[e : e + 1, :]).astype(jnp.int32)
            s = pl.multiple_of((base[e] // 16) * 16, 16)
            start.append(s)
            off.append(base[e] - s)
            need.append(off[e] + count)
            base[e] = base[e] + count
        n_win = jnp.maximum(1, (jnp.maximum(need[0], need[1]) + WIN - 1) // WIN)
        first.append(start)
        skew.append(off)
        wins.append(n_win)

        def select(k, carry, place=place, start=start, off=off, rows=rows):
            chosen = [
                jnp.where(place[e : e + 1, :] + (off[e] - k * WIN) == slot_row, 1.0, 0.0)
                for e in range(2)
            ]
            chosen = jnp.concatenate(chosen, axis=0).astype(BF)
            for lo in range(0, width + META, 512):
                hi = min(lo + 512, width + META)
                got = jnp.dot(chosen, x_s[rows, lo:hi], preferred_element_type=F32).astype(BF)
                for e in range(2):
                    to = pl.ds(pl.multiple_of(start[e] + k * WIN, 16), WIN)
                    sel_s[e, to, lo:hi] = sel_s[e, to, lo:hi] + got[e * WIN : (e + 1) * WIN]
            return carry

        lax.fori_loop(0, n_win, select, 0)

    for e in range(2):
        for j in range(3):
            w_copies[3 * e + j].wait()

        def rows_of(m, carry, e=e):
            rows = pl.ds(pl.multiple_of(m * mb, mb), mb)

            def up(n, carry):
                cols = pl.ds(pl.multiple_of(n * 256, 256), 256)
                x = sel_s[e, rows, :width]
                g = jnp.dot(x, wg_s[e, :, cols], preferred_element_type=F32)
                u = jnp.dot(x, wu_s[e, :, cols], preferred_element_type=F32)
                hid_s[:, cols] = (g / (1.0 + jnp.exp(-g)) * u).astype(BF)
                return carry

            lax.fori_loop(0, hid // 256, up, 0)
            num = jnp.dot(sel_s[e, rows, width:], pick_col, preferred_element_type=F32)
            gate = num[:, e : e + 1] * (1.0 / GATE_DEN)

            def down(n, carry):
                cols = pl.ds(pl.multiple_of(n * 256, 256), 256)
                y = jnp.dot(hid_s[...], wd_s[e, :, cols], preferred_element_type=F32)
                y_s[e, rows, cols] = (y * gate).astype(BF)
                return carry

            lax.fori_loop(0, width // 256, down, 0)
            return carry

        lax.fori_loop(0, (base[e] + mb - 1) // mb, rows_of, 0)

    for b in range(n_block):
        rows = pl.ds(b * block, block)
        num = jnp.dot(x_s[rows, width:], pick_col, preferred_element_type=F32)
        hit = jnp.where(num > 0.0, 1.0, 0.0)
        rank = jnp.dot(lower, hit.astype(BF), preferred_element_type=F32)
        place = jnp.where(num > 0.0, rank - 1.0, -1.0e4).astype(jnp.int32)

        def back(k, b=b, place=place):
            spread = [
                jnp.where(place[:, e : e + 1] + (skew[b][e] - k * WIN) == slot_col, 1.0, 0.0)
                for e in range(2)
            ]
            spread = jnp.concatenate(spread, axis=1).astype(BF)
            for lo in range(0, width, 512):
                y = jnp.concatenate(
                    [
                        y_s[e, pl.ds(pl.multiple_of(first[b][e] + k * WIN, 16), WIN), lo : lo + 512]
                        for e in range(2)
                    ],
                    axis=0,
                )
                yield lo, jnp.dot(spread, y, preferred_element_type=F32)

        @pl.when(wins[b] == 1)
        def _(rows=rows, back=back):
            for lo, part in back(0):
                out_s[rows, lo : lo + 512] = part.astype(BF)

        @pl.when(wins[b] > 1)
        def _(b=b, rows=rows, back=back):
            acc_s[...] = jnp.zeros(acc_s.shape, F32)

            def more(k, carry):
                for lo, part in back(k):
                    acc_s[:, lo : lo + 512] = acc_s[:, lo : lo + 512] + part
                return carry

            lax.fori_loop(0, wins[b], more, 0)
            out_s[rows, :] = acc_s[...].astype(BF)

        for i in range(n_piece):
            if b * block < starts[i] + piece_rows[i] <= (b + 1) * block:
                pltpu.make_async_copy(
                    out_s.at[pl.ds(starts[i], piece_rows[i])], outs[i], o_sem.at[i]
                ).start()
    for i in range(n_piece):
        pltpu.make_async_copy(
            out_s.at[pl.ds(starts[i], piece_rows[i])], outs[i], o_sem.at[i]
        ).wait()


def apply_experts(ids, pieces, weights, most, mb):
    piece_rows = tuple(p.shape[0] for p in pieces)
    total = sum(piece_rows)
    width = pieces[0].shape[1] - META
    hid = weights[0].shape[2]
    block = 256
    rows_cap = -(-(most + 2 * WIN) // mb) * mb
    n = len(pieces)
    slots = 2 * most
    return pl.pallas_call(
        functools.partial(expert_kernel, piece_rows, block, mb, rows_cap, width),
        out_shape=[jax.ShapeDtypeStruct((r, width), BF) for r in piece_rows],
        in_specs=[pl.BlockSpec(memory_space=pltpu.SMEM)]
        + [pl.BlockSpec(memory_space=pl.ANY)] * (n + 6),
        out_specs=[pl.BlockSpec(memory_space=pl.ANY)] * n,
        scratch_shapes=[
            pltpu.VMEM((total, width + META), BF),
            pltpu.VMEM((2, rows_cap, width + META), BF),
            pltpu.VMEM((mb, hid), BF),
            pltpu.VMEM((2, rows_cap, width), BF),
            pltpu.VMEM((block, width), F32),
            pltpu.VMEM((total, width), BF),
            pltpu.VMEM((2, width, hid), BF),
            pltpu.VMEM((2, width, hid), BF),
            pltpu.VMEM((2, hid, width), BF),
            pltpu.SemaphoreType.DMA((n,)),
            pltpu.SemaphoreType.DMA((6,)),
            pltpu.SemaphoreType.DMA((n,)),
        ],
        compiler_params=pltpu.CompilerParams(vmem_limit_bytes=56 * 1024 * 1024),
        cost_estimate=pl.CostEstimate(
            flops=2 * slots * 3 * width * hid,
            bytes_accessed=2 * (6 * width * hid + 2 * total * width),
            transcendentals=slots * hid,
        ),
    )(ids, *pieces, *weights)


def add(*xs):
    total = xs[0].astype(F32)
    for x in xs[1:]:
        total = total + x.astype(F32)
    return total.astype(BF)


def to_next(x, axis):
    return lax.ppermute(x, axis, NEXT)


def to_prev(x, axis):
    return lax.ppermute(x, axis, PREV)


def near(streams):
    return [(to_next(x, axis), to_prev(x, axis)) for x, axis in streams]


def far(got, streams):
    n = got[0][0].shape[0] // 2
    return [
        (to_next(p[:n], axis), to_prev(q[n:], axis))
        for (p, q), (x, axis) in zip(got, streams)
    ]


def reduce_first(parts, axes):
    one = [(to_next(p[1][1], ax), to_prev(p[3][0], ax)) for p, ax in zip(parts, axes)]
    two = [(to_next(p[2][0], ax), to_prev(p[2][1], ax)) for p, ax in zip(parts, axes)]
    three = [
        (to_next(add(p[1][0], a), ax), to_prev(add(p[3][1], b), ax))
        for p, ax, (a, b) in zip(parts, axes, two)
    ]
    return [
        (add(p[0][0], c, b), add(p[0][1], a, d))
        for p, (a, b), (c, d) in zip(parts, one, three)
    ]


def reduce_second(parts, axes):
    n = parts[0][0].shape[0] // 2
    one = [(to_next(p[2][:n], ax), to_prev(p[2][n:], ax)) for p, ax in zip(parts, axes)]
    two = [
        (
            to_next(jnp.concatenate([add(p[1][:n], a), p[1][n:]]), ax),
            to_prev(jnp.concatenate([p[3][:n], add(p[3][n:], b)]), ax),
        )
        for p, ax, (a, b) in zip(parts, axes, one)
    ]
    return [add(p[0], a, b) for p, (a, b) in zip(parts, two)]


def body(tokens, routes, gate_num, w_gate, w_up, w_down):
    half = tokens.shape[0] // 2
    own = lax.axis_index(("x", "y", "core"))
    ids = jnp.stack([own, own ^ 1]).astype(jnp.int32)
    swap = [(0, 1), (1, 0)]

    experts = jnp.arange(32, dtype=jnp.int32)
    num = jnp.sum(jnp.where(routes[:, :, None] == experts, gate_num[:, :, None], 0), axis=1)
    meta = jnp.concatenate(
        [num >> 2, num & 3, jnp.zeros((tokens.shape[0], META - 64), jnp.int32)], axis=1
    )
    rows = jnp.concatenate([tokens, meta.astype(BF)], axis=1)

    streams = [(rows[:half], "x"), (rows[half:], "y")]
    got = near(streams)
    p_gate = lax.ppermute(w_gate, "core", swap)
    got, p_gate = lax.optimization_barrier((got, p_gate))
    opp = far(got, streams)
    p_up = lax.ppermute(w_up, "core", swap)
    opp, p_up = lax.optimization_barrier((opp, p_up))
    cat = [
        jnp.concatenate([x, p, q, *o]) for (x, axis), (p, q), o in zip(streams, got, opp)
    ]
    streams = [(cat[0], "y"), (cat[1], "x")]
    axes = ["y", "x"]
    got = near(streams)
    p_down = lax.ppermute(w_down, "core", swap)
    weights = (w_gate, w_up, w_down, p_gate, p_up, p_down)
    most = 40 * 8
    here = apply_experts(ids, cat, weights, most, 192)
    opp = far(got, streams)
    beside = apply_experts(ids, [*got[0], *got[1]], weights, 2 * most, 384)
    across = apply_experts(ids, [*opp[0], *opp[1]], weights, most, 192)

    def halves(x):
        n = x.shape[0] // 2
        return x[:n], x[n:]

    parts = [
        {
            0: halves(here[i]),
            3: halves(beside[2 * i]),
            1: halves(beside[2 * i + 1]),
            2: (across[2 * i], across[2 * i + 1]),
        }
        for i in range(2)
    ]
    sums = reduce_first(parts, axes)
    second = []
    for h0, h1 in sums:
        second.append({0: h0[:half], 3: h0[half:], 1: h1[:half], 2: h1[half:]})
    return jnp.concatenate(reduce_second(second, ["x", "y"]))


def solution(mesh):
    fine = Mesh(
        mesh.devices.reshape(mesh.shape["dp"], RING, RING, 2), ("dp", "x", "y", "core")
    )
    rows = P(("dp", "x", "y", "core"), None)
    expert = P(("x", "y", "core"), None, None)
    return jax.shard_map(
        body,
        mesh=fine,
        in_specs=(rows, rows, rows, expert, expert, expert),
        out_specs=rows,
        check_vma=False,
    )
```

```python
import functools

import jax
import jax.numpy as jnp
from jax import lax
from jax.experimental import pallas as pl
from jax.experimental.pallas import tpu as pltpu
from jax.sharding import Mesh, PartitionSpec as P

GATE_DEN = 1024
META = 128
WIN = 128
OUT = 128
STEP = 512
COST = 1000
UP = 256
DOWN = 512
VMEM_LIMIT = 26 * 1024 * 1024
BF = jnp.bfloat16
F32 = jnp.float32
RING = 4
NEXT = [(i, (i + 1) % RING) for i in range(RING)]
PREV = [(i, (i + RING - 1) % RING) for i in range(RING)]
ACROSS = [(i, (i + 2) % RING) for i in range(RING)]


def expert_kernel(piece_rows, block, mb, rows_cap, width, ids, *refs):
    n_piece = len(piece_rows)
    pieces, refs = refs[:n_piece], refs[n_piece:]
    weights, refs = refs[:6], refs[6:]
    n_out = sum(piece_rows) // OUT
    outs, refs = refs[:n_out], refs[n_out:]
    sel_s, hid_s, wg_s, wu_s, wd_s, w_sem = refs
    w_copies = [
        pltpu.make_async_copy(weights[3 + j], dst, w_sem.at[j])
        for j, dst in enumerate((wg_s, wu_s, wd_s))
    ]
    for c in w_copies:
        c.start()
    total = sum(piece_rows)
    n_block = total // block
    hid = weights[0].shape[2]
    cut = []
    for i in range(n_piece):
        if cut and sum(piece_rows[j] for j in cut[-1]) < block:
            cut[-1].append(i)
        else:
            cut.append([i])

    def load(b, lo, hi):
        parts = [pieces[i][:, lo:hi] for i in cut[b]]
        return parts[0] if len(parts) == 1 else jnp.concatenate(parts, axis=0)

    def save(b, lo, hi, value):
        for i in range(block // OUT):
            outs[b * (block // OUT) + i][:, lo:hi] = value[i * OUT : (i + 1) * OUT]

    sel_s[...] = jnp.zeros(sel_s.shape, BF)

    def pick(shape, expert_axis):
        col = lax.broadcasted_iota(jnp.int32, shape, 1 - expert_axis)
        which = lax.broadcasted_iota(jnp.int32, shape, expert_axis)
        mine = jnp.where(which == 0, ids[0], ids[1])
        high = jnp.where(col == mine, 4.0, 0.0)
        low = jnp.where(col == mine + 32, 1.0, 0.0)
        return jnp.where(which < 2, high + low, 0.0).astype(BF)

    pick_row = pick((8, META), 0)
    pick_col = pick((META, META), 1)
    lane = lax.broadcasted_iota(jnp.int32, (block, block), 1)
    sub = lax.broadcasted_iota(jnp.int32, (block, block), 0)
    upper = jnp.where(sub <= lane, 1.0, 0.0).astype(BF)
    lower = jnp.where(lane <= sub, 1.0, 0.0).astype(BF)
    slot_row = lax.broadcasted_iota(jnp.int32, (WIN, block), 0)
    slot_col = lax.broadcasted_iota(jnp.int32, (block, WIN), 1)

    base = [jnp.int32(0), jnp.int32(0)]
    first, skew, wins, places = [], [], [], []
    for b in range(n_block):
        meta = load(b, width, width + META)
        num = lax.dot_general(pick_row, meta, (((1,), (1,)), ((), ())), preferred_element_type=F32)
        hit = jnp.where(num > 0.0, 1.0, 0.0)
        rank = jnp.dot(hit.astype(BF), upper, preferred_element_type=F32)
        places.append(jnp.where(num > 0.0, rank - 1.0, -1.0e4).astype(jnp.int32))
        start, off, need = [], [], []
        for e in range(2):
            count = jnp.sum(hit[e : e + 1, :]).astype(jnp.int32)
            s = pl.multiple_of((base[e] // 16) * 16, 16)
            start.append(s)
            off.append(base[e] - s)
            need.append(off[e] + count)
            base[e] = base[e] + count
        first.append(start)
        skew.append(off)
        wins.append(jnp.maximum(1, (jnp.maximum(need[0], need[1]) + WIN - 1) // WIN))
    single = functools.reduce(jnp.maximum, wins) == 1

    def select(b, k):
        chosen = [
            jnp.where(places[b][e : e + 1, :] + (skew[b][e] - k * WIN) == slot_row, 1.0, 0.0)
            for e in range(2)
        ]
        chosen = jnp.concatenate(chosen, axis=0).astype(BF)
        for lo in range(0, width + META, 512):
            hi = min(lo + 512, width + META)
            got = jnp.dot(chosen, load(b, lo, hi), preferred_element_type=F32).astype(BF)
            for e in range(2):
                to = pl.ds(pl.multiple_of(first[b][e] + k * WIN, 16), WIN)
                sel_s[e, to, lo:hi] = sel_s[e, to, lo:hi] + got[e * WIN : (e + 1) * WIN]

    @pl.when(single)
    def _():
        for b in range(n_block):
            select(b, 0)

    @pl.when(jnp.logical_not(single))
    def _():
        for b in range(n_block):

            def one(k, carry, b=b):
                select(b, k)
                return carry

            lax.fori_loop(0, wins[b], one, 0)

    for e in range(2):
        if e == 0:
            wg, wu, wd = weights[:3]
        else:
            wg, wu, wd = wg_s, wu_s, wd_s
            for c in w_copies:
                c.wait()

        def rows_of(m, carry, e=e, wg=wg, wu=wu, wd=wd):
            rows = pl.ds(pl.multiple_of(m * mb, mb), mb)

            for lo in range(0, hid, UP):
                x = sel_s[e, rows, :width]
                g = jnp.dot(x, wg[0, :, lo : lo + UP], preferred_element_type=F32)
                u = jnp.dot(x, wu[0, :, lo : lo + UP], preferred_element_type=F32)
                hid_s[:, lo : lo + UP] = (g / (1.0 + jnp.exp(-g)) * u).astype(BF)
            num = jnp.dot(sel_s[e, rows, width:], pick_col, preferred_element_type=F32)
            gate = num[:, e : e + 1] * (1.0 / GATE_DEN)

            for lo in range(0, width, DOWN):
                y = jnp.dot(hid_s[...], wd[0, :, lo : lo + DOWN], preferred_element_type=F32)
                sel_s[e, rows, lo : lo + DOWN] = (y * gate).astype(BF)
            return carry

        lax.fori_loop(0, (base[e] + mb - 1) // mb, rows_of, 0)

    columns = []
    for b in range(n_block):
        num = jnp.dot(load(b, width, width + META), pick_col, preferred_element_type=F32)
        hit = jnp.where(num > 0.0, 1.0, 0.0)
        rank = jnp.dot(lower, hit.astype(BF), preferred_element_type=F32)
        columns.append(jnp.where(num > 0.0, rank - 1.0, -1.0e4).astype(jnp.int32))

    def spread(b, k):
        hot = [
            jnp.where(columns[b][:, e : e + 1] + (skew[b][e] - k * WIN) == slot_col, 1.0, 0.0)
            for e in range(2)
        ]
        return jnp.concatenate(hot, axis=1).astype(BF)

    def put(b, k, lo, hot):
        y = jnp.concatenate(
            [
                sel_s[e, pl.ds(pl.multiple_of(first[b][e] + k * WIN, 16), WIN), lo : lo + STEP]
                for e in range(2)
            ],
            axis=0,
        )
        return jnp.dot(hot, y, preferred_element_type=F32)

    @pl.when(single)
    def _():
        for b in range(n_block):
            hot = spread(b, 0)
            for lo in range(0, width, STEP):
                save(b, lo, lo + STEP, put(b, 0, lo, hot).astype(BF))

    @pl.when(jnp.logical_not(single))
    def _():
        for b in range(n_block):
            for lo in range(0, width, STEP):

                def more(k, total, b=b, lo=lo):
                    return total + put(b, k, lo, spread(b, k))

                part = lax.fori_loop(0, wins[b], more, jnp.zeros((block, STEP), F32))
                save(b, lo, lo + STEP, part.astype(BF))


def in_vmem(x):
    return pltpu.with_memory_space_constraint(x, pltpu.VMEM)


def apply_experts(ids, pieces, weights, most, mb):
    piece_rows = tuple(p.shape[0] for p in pieces)
    total = sum(piece_rows)
    width = pieces[0].shape[1] - META
    hid = weights[0].shape[2]
    block = 256
    rows_cap = most + 2 * WIN
    n, n_out = len(pieces), total // OUT
    slots = 2 * most
    return pl.pallas_call(
        functools.partial(expert_kernel, piece_rows, block, mb, rows_cap, width),
        out_shape=[jax.ShapeDtypeStruct((OUT, width), BF)] * n_out,
        in_specs=[pl.BlockSpec(memory_space=pltpu.SMEM)]
        + [pl.BlockSpec(memory_space=pltpu.VMEM)] * (n + 3)
        + [pl.BlockSpec(memory_space=pltpu.HBM)] * 3,
        out_specs=[pl.BlockSpec(memory_space=pltpu.VMEM)] * n_out,
        scratch_shapes=[
            pltpu.VMEM((2, rows_cap, width + META), BF),
            pltpu.VMEM((mb, hid), BF),
            pltpu.VMEM((1, width, hid), BF),
            pltpu.VMEM((1, width, hid), BF),
            pltpu.VMEM((1, hid, width), BF),
            pltpu.SemaphoreType.DMA((3,)),
        ],
        compiler_params=pltpu.CompilerParams(vmem_limit_bytes=VMEM_LIMIT),
        cost_estimate=pl.CostEstimate(flops=slots * COST, bytes_accessed=0, transcendentals=0),
    )(ids, *[in_vmem(p) for p in pieces], *weights)


def add(*xs):
    total = xs[0].astype(F32)
    for x in xs[1:]:
        total = total + x.astype(F32)
    return total.astype(BF)


def to_next(x, axis):
    return lax.ppermute(x, axis, NEXT)


def to_prev(x, axis):
    return lax.ppermute(x, axis, PREV)


def near(streams):
    return [(to_next(x, axis), to_prev(x, axis)) for x, axis in streams]


def far(got, streams):
    n = got[0][0].shape[0] // 2
    return [
        (to_next(p[:n], axis), to_prev(q[n:], axis))
        for (p, q), (x, axis) in zip(got, streams)
    ]


def reduce_first(parts, axes):
    one = [(to_next(p[1][1], ax), to_prev(p[3][0], ax)) for p, ax in zip(parts, axes)]
    two = []
    for i, (p, ax) in enumerate(zip(parts, axes)):
        a, x = lax.optimization_barrier((one[i][0], p[2][0]))
        b, y = lax.optimization_barrier((one[i][1], p[2][1]))
        one[i] = (a, b)
        two.append((to_next(x, ax), to_prev(y, ax)))
    three = [
        (to_next(add(p[1][0], a), ax), to_prev(add(p[3][1], b), ax))
        for p, ax, (a, b) in zip(parts, axes, two)
    ]
    return [
        (add(p[0][0], c, b), add(p[0][1], a, d))
        for p, (a, b), (c, d) in zip(parts, one, three)
    ]


def body(tokens, routes, gate_num, w_gate, w_up, w_down):
    half = tokens.shape[0] // 2
    own = lax.axis_index(("x", "y", "core"))
    ids = jnp.stack([own, own ^ 1]).astype(jnp.int32)
    swap = [(0, 1), (1, 0)]

    experts = jnp.arange(32, dtype=jnp.int32)
    num = jnp.sum(jnp.where(routes[:, :, None] == experts, gate_num[:, :, None], 0), axis=1)
    meta = jnp.concatenate(
        [num >> 2, num & 3, jnp.zeros((tokens.shape[0], META - 64), jnp.int32)], axis=1
    )
    rows = jnp.concatenate([tokens, meta.astype(BF)], axis=1)

    streams = [(rows[:half], "x"), (rows[half:], "y")]
    p_gate = lax.ppermute(w_gate, "core", swap)
    p_up = lax.ppermute(w_up, "core", swap)
    got = near(streams)
    cat = []
    for i, ((p, q), (x, axis)) in enumerate(zip(got, streams)):
        late = lax.optimization_barrier((x, got[1 - i][0]))[0]
        cat.append(jnp.concatenate([x, p, q, lax.ppermute(late, axis, ACROSS)]))
    cat, p_gate, p_up, w_down_late = lax.optimization_barrier((cat, p_gate, p_up, w_down))
    axes = ["y", "x"]
    streams = [(x, axis) for x, axis in zip(cat, axes)]
    got = near(streams)
    p_down = lax.ppermute(w_down_late, "core", swap)
    weights = [in_vmem(w) for w in (w_gate, w_up, w_down)] + [p_gate, p_up, p_down]
    most = 40 * 8
    here = apply_experts(ids, cat, weights, most, 192)
    here, got = lax.optimization_barrier((here, got))
    opp = far(got, streams)
    beside = apply_experts(ids, [*got[0], *got[1]], weights, 2 * most, 384)
    beside, opp = lax.optimization_barrier((beside, opp))
    across = apply_experts(ids, [*opp[0], *opp[1]], weights, most, 192)
    parts = [
        {
            0: here[2 * i : 2 * i + 2],
            3: beside[4 * i : 4 * i + 2],
            1: beside[4 * i + 2 : 4 * i + 4],
            2: across[2 * i : 2 * i + 2],
        }
        for i in range(2)
    ]
    sums = []
    for (h0, h1), axis in zip(reduce_first(parts, axes), ["x", "y"]):
        sums.append(
            add(
                h0[:half],
                to_prev(h0[half:], axis),
                to_next(h1[:half], axis),
                lax.ppermute(h1[half:], axis, ACROSS),
            )
        )
    return jnp.concatenate(sums)


def solution(mesh):
    fine = Mesh(
        mesh.devices.reshape(mesh.shape["dp"], RING, RING, 2), ("dp", "x", "y", "core")
    )
    rows = P(("dp", "x", "y", "core"), None)
    expert = P(("x", "y", "core"), None, None)
    return jax.shard_map(
        body,
        mesh=fine,
        in_specs=(rows, rows, rows, expert, expert, expert),
        out_specs=rows,
        check_vma=False,
    )
```

```python
import functools

import jax
import jax.numpy as jnp
from jax import lax
from jax.experimental import pallas as pl
from jax.experimental.pallas import tpu as pltpu
from jax.sharding import Mesh, PartitionSpec as P

GATE_DEN = 1024
META = 128
WIN = 128
OUT = 128
STEP = 512
COST = 1000
UP = 256
DOWN = 512
VMEM_LIMIT = 26 * 1024 * 1024
BF = jnp.bfloat16
F32 = jnp.float32
RING = 4
NEXT = [(i, (i + 1) % RING) for i in range(RING)]
PREV = [(i, (i + RING - 1) % RING) for i in range(RING)]
ACROSS = [(i, (i + 2) % RING) for i in range(RING)]


def expert_kernel(piece_rows, block, mb, rows_cap, width, ids, *refs):
    n_piece = len(piece_rows)
    pieces, refs = refs[:n_piece], refs[n_piece:]
    weights, refs = refs[:6], refs[6:]
    n_out = sum(piece_rows) // OUT
    outs, refs = refs[:n_out], refs[n_out:]
    sel_s, hid_s, wg_s, wu_s, wd_s, w_sem = refs
    w_copies = [
        pltpu.make_async_copy(weights[3 + j], dst, w_sem.at[j])
        for j, dst in enumerate((wg_s, wu_s, wd_s))
    ]
    for c in w_copies:
        c.start()
    total = sum(piece_rows)
    n_block = total // block
    hid = weights[0].shape[2]
    cut = []
    for i in range(n_piece):
        if cut and sum(piece_rows[j] for j in cut[-1]) < block:
            cut[-1].append(i)
        else:
            cut.append([i])

    def load(b, lo, hi):
        parts = [pieces[i][:, lo:hi] for i in cut[b]]
        return parts[0] if len(parts) == 1 else jnp.concatenate(parts, axis=0)

    def save(b, lo, hi, value):
        for i in range(block // OUT):
            outs[b * (block // OUT) + i][:, lo:hi] = value[i * OUT : (i + 1) * OUT]

    sel_s[...] = jnp.zeros(sel_s.shape, BF)

    def pick(shape, expert_axis):
        col = lax.broadcasted_iota(jnp.int32, shape, 1 - expert_axis)
        which = lax.broadcasted_iota(jnp.int32, shape, expert_axis)
        mine = jnp.where(which == 0, ids[0], ids[1])
        high = jnp.where(col == mine, 4.0, 0.0)
        low = jnp.where(col == mine + 32, 1.0, 0.0)
        return jnp.where(which < 2, high + low, 0.0).astype(BF)

    pick_row = pick((8, META), 0)
    pick_col = pick((META, META), 1)
    lane = lax.broadcasted_iota(jnp.int32, (block, block), 1)
    sub = lax.broadcasted_iota(jnp.int32, (block, block), 0)
    upper = jnp.where(sub <= lane, 1.0, 0.0).astype(BF)
    lower = jnp.where(lane <= sub, 1.0, 0.0).astype(BF)
    slot_row = lax.broadcasted_iota(jnp.int32, (WIN, block), 0)
    slot_col = lax.broadcasted_iota(jnp.int32, (block, WIN), 1)

    base = [jnp.int32(0), jnp.int32(0)]
    first, skew, wins, places = [], [], [], []
    for b in range(n_block):
        meta = load(b, width, width + META)
        num = lax.dot_general(pick_row, meta, (((1,), (1,)), ((), ())), preferred_element_type=F32)
        hit = jnp.where(num > 0.0, 1.0, 0.0)
        rank = jnp.dot(hit.astype(BF), upper, preferred_element_type=F32)
        places.append(jnp.where(num > 0.0, rank - 1.0, -1.0e4).astype(jnp.int32))
        start, off, need = [], [], []
        for e in range(2):
            count = jnp.sum(hit[e : e + 1, :]).astype(jnp.int32)
            s = pl.multiple_of((base[e] // 16) * 16, 16)
            start.append(s)
            off.append(base[e] - s)
            need.append(off[e] + count)
            base[e] = base[e] + count
        first.append(start)
        skew.append(off)
        wins.append(jnp.maximum(1, (jnp.maximum(need[0], need[1]) + WIN - 1) // WIN))
    single = functools.reduce(jnp.maximum, wins) == 1

    def select(b, k):
        chosen = [
            jnp.where(places[b][e : e + 1, :] + (skew[b][e] - k * WIN) == slot_row, 1.0, 0.0)
            for e in range(2)
        ]
        chosen = jnp.concatenate(chosen, axis=0).astype(BF)
        for lo in range(0, width + META, 512):
            hi = min(lo + 512, width + META)
            got = jnp.dot(chosen, load(b, lo, hi), preferred_element_type=F32).astype(BF)
            for e in range(2):
                to = pl.ds(pl.multiple_of(first[b][e] + k * WIN, 16), WIN)
                sel_s[e, to, lo:hi] = sel_s[e, to, lo:hi] + got[e * WIN : (e + 1) * WIN]

    @pl.when(single)
    def _():
        for b in range(n_block):
            select(b, 0)

    @pl.when(jnp.logical_not(single))
    def _():
        for b in range(n_block):

            def one(k, carry, b=b):
                select(b, k)
                return carry

            lax.fori_loop(0, wins[b], one, 0)

    for e in range(2):
        if e == 0:
            wg, wu, wd = weights[:3]
        else:
            wg, wu, wd = wg_s, wu_s, wd_s
            for c in w_copies:
                c.wait()

        def rows_of(m, carry, e=e, wg=wg, wu=wu, wd=wd):
            rows = pl.ds(pl.multiple_of(m * mb, mb), mb)

            for lo in range(0, hid, UP):
                x = sel_s[e, rows, :width]
                g = jnp.dot(x, wg[0, :, lo : lo + UP], preferred_element_type=F32)
                u = jnp.dot(x, wu[0, :, lo : lo + UP], preferred_element_type=F32)
                hid_s[:, lo : lo + UP] = (g / (1.0 + jnp.exp(-g)) * u).astype(BF)
            num = jnp.dot(sel_s[e, rows, width:], pick_col, preferred_element_type=F32)
            gate = num[:, e : e + 1] * (1.0 / GATE_DEN)

            for lo in range(0, width, DOWN):
                y = jnp.dot(hid_s[...], wd[0, :, lo : lo + DOWN], preferred_element_type=F32)
                sel_s[e, rows, lo : lo + DOWN] = (y * gate).astype(BF)
            return carry

        lax.fori_loop(0, (base[e] + mb - 1) // mb, rows_of, 0)

    columns = []
    for b in range(n_block):
        num = jnp.dot(load(b, width, width + META), pick_col, preferred_element_type=F32)
        hit = jnp.where(num > 0.0, 1.0, 0.0)
        rank = jnp.dot(lower, hit.astype(BF), preferred_element_type=F32)
        columns.append(jnp.where(num > 0.0, rank - 1.0, -1.0e4).astype(jnp.int32))

    def spread(b, k):
        hot = [
            jnp.where(columns[b][:, e : e + 1] + (skew[b][e] - k * WIN) == slot_col, 1.0, 0.0)
            for e in range(2)
        ]
        return jnp.concatenate(hot, axis=1).astype(BF)

    def put(b, k, lo, hot):
        y = jnp.concatenate(
            [
                sel_s[e, pl.ds(pl.multiple_of(first[b][e] + k * WIN, 16), WIN), lo : lo + STEP]
                for e in range(2)
            ],
            axis=0,
        )
        return jnp.dot(hot, y, preferred_element_type=F32)

    @pl.when(single)
    def _():
        for b in range(n_block):
            hot = spread(b, 0)
            for lo in range(0, width, STEP):
                save(b, lo, lo + STEP, put(b, 0, lo, hot).astype(BF))

    @pl.when(jnp.logical_not(single))
    def _():
        for b in range(n_block):
            for lo in range(0, width, STEP):

                def more(k, total, b=b, lo=lo):
                    return total + put(b, k, lo, spread(b, k))

                part = lax.fori_loop(0, wins[b], more, jnp.zeros((block, STEP), F32))
                save(b, lo, lo + STEP, part.astype(BF))


def in_vmem(x):
    return pltpu.with_memory_space_constraint(x, pltpu.VMEM)


def apply_experts(ids, pieces, weights):
    piece_rows = tuple(p.shape[0] for p in pieces)
    total = sum(piece_rows)
    width = pieces[0].shape[1] - META
    hid = weights[0].shape[2]
    block = 256
    most = 40 * (total // 64)
    mb = 192
    rows_cap = most + 2 * WIN
    n, n_out = len(pieces), total // OUT
    slots = 2 * most
    return pl.pallas_call(
        functools.partial(expert_kernel, piece_rows, block, mb, rows_cap, width),
        out_shape=[jax.ShapeDtypeStruct((OUT, width), BF)] * n_out,
        in_specs=[pl.BlockSpec(memory_space=pltpu.SMEM)]
        + [pl.BlockSpec(memory_space=pltpu.VMEM)] * (n + 3)
        + [pl.BlockSpec(memory_space=pltpu.HBM)] * 3,
        out_specs=[pl.BlockSpec(memory_space=pltpu.VMEM)] * n_out,
        scratch_shapes=[
            pltpu.VMEM((2, rows_cap, width + META), BF),
            pltpu.VMEM((mb, hid), BF),
            pltpu.VMEM((1, width, hid), BF),
            pltpu.VMEM((1, width, hid), BF),
            pltpu.VMEM((1, hid, width), BF),
            pltpu.SemaphoreType.DMA((3,)),
        ],
        compiler_params=pltpu.CompilerParams(vmem_limit_bytes=VMEM_LIMIT),
        cost_estimate=pl.CostEstimate(flops=slots * COST, bytes_accessed=0, transcendentals=0),
    )(ids, *[in_vmem(p) for p in pieces], *weights)


def add(*xs):
    total = xs[0].astype(F32)
    for x in xs[1:]:
        total = total + x.astype(F32)
    return total.astype(BF)


def to_next(x, axis):
    return lax.ppermute(x, axis, NEXT)


def to_prev(x, axis):
    return lax.ppermute(x, axis, PREV)


def near(streams):
    return [(to_next(x, axis), to_prev(x, axis)) for x, axis in streams]


def after(x, *first):
    return lax.optimization_barrier((x, first))[0]


def body(tokens, routes, gate_num, w_gate, w_up, w_down):
    half = tokens.shape[0] // 2
    own = lax.axis_index(("x", "y", "core"))
    ids = jnp.stack([own, own ^ 1]).astype(jnp.int32)
    swap = [(0, 1), (1, 0)]

    experts = jnp.arange(32, dtype=jnp.int32)
    num = jnp.sum(jnp.where(routes[:, :, None] == experts, gate_num[:, :, None], 0), axis=1)
    meta = jnp.concatenate(
        [num >> 2, num & 3, jnp.zeros((tokens.shape[0], META - 64), jnp.int32)], axis=1
    )
    rows = jnp.concatenate([tokens, meta.astype(BF)], axis=1)

    streams = [(rows[:half], "x"), (rows[half:], "y")]
    p_gate = lax.ppermute(w_gate, "core", swap)
    p_up = lax.ppermute(w_up, "core", swap)
    got = near(streams)
    halves = []
    for i, ((p, q), (x, axis)) in enumerate(zip(got, streams)):
        late = lax.optimization_barrier((x, got[1 - i][0]))[0]
        o = lax.ppermute(late, axis, ACROSS)
        halves.append((jnp.concatenate([x, p]), jnp.concatenate([q, o])))
    halves, p_gate, p_up, w_down_late = lax.optimization_barrier((halves, p_gate, p_up, w_down))
    p_down = lax.ppermute(w_down_late, "core", swap)
    weights = [in_vmem(w) for w in (w_gate, w_up, w_down)] + [p_gate, p_up, p_down]
    axes = ["y", "x"]
    one = [(to_next(h0, ax), to_prev(h1, ax)) for (h0, h1), ax in zip(halves, axes)]
    here = apply_experts(ids, [*halves[0], *halves[1]], weights)
    two = []
    for (a, b), (h0, h1), ax in zip(one, halves, axes):
        two.append((to_next(after(h1, a, here), ax), to_prev(after(h0, b, here), ax)))
    early = apply_experts(ids, [*one[0], *one[1]], weights)
    opp = []
    for (a, b), (c, d), ax in zip(one, two, axes):
        opp.append((to_next(after(a, c, early), ax), to_prev(after(b, d, early), ax)))
    gone = []
    for i, ((a, b), ax) in enumerate(zip(opp, axes)):
        gone.append(
            (to_next(after(early[2 * i + 1], a), ax), to_prev(after(early[2 * i], b), ax))
        )
    across = apply_experts(ids, [*opp[0], *opp[1]], weights)
    late = apply_experts(ids, after([*two[0], *two[1]], gone, across), weights)
    passed = []
    for i, ((a, b), ax) in enumerate(zip(gone, axes)):
        passed.append(
            (to_next(after(across[2 * i], a), ax), to_prev(after(across[2 * i + 1], b), ax))
        )
    firsts = []
    for i, ((a, b), (f, g), ax) in enumerate(zip(gone, passed, axes)):
        c = to_next(add(late[2 * i + 1], f), ax)
        d = to_prev(add(late[2 * i], g), ax)
        firsts.append((add(here[2 * i], c, b), add(here[2 * i + 1], a, d)))
    sums = []
    for (h0, h1), axis in zip(firsts, ["x", "y"]):
        sums.append(
            add(
                h0[:half],
                to_prev(h0[half:], axis),
                to_next(h1[:half], axis),
                lax.ppermute(h1[half:], axis, ACROSS),
            )
        )
    return jnp.concatenate(sums)


def solution(mesh):
    fine = Mesh(
        mesh.devices.reshape(mesh.shape["dp"], RING, RING, 2), ("dp", "x", "y", "core")
    )
    rows = P(("dp", "x", "y", "core"), None)
    expert = P(("x", "y", "core"), None, None)
    return jax.shard_map(
        body,
        mesh=fine,
        in_specs=(rows, rows, rows, expert, expert, expert),
        out_specs=rows,
        check_vma=False,
    )
```

```python
import functools

import jax
import jax.numpy as jnp
from jax import lax
from jax.experimental import pallas as pl
from jax.experimental.pallas import tpu as pltpu
from jax.sharding import Mesh, PartitionSpec as P

GATE_DEN = 1024
META = 128
WIN = 128
OUT = 128
STEP = 512
COST = 1000
UP = 256
DOWN = 512
VMEM_LIMIT = 26 * 1024 * 1024
BF = jnp.bfloat16
F32 = jnp.float32
RING = 4
NEXT = [(i, (i + 1) % RING) for i in range(RING)]
PREV = [(i, (i + RING - 1) % RING) for i in range(RING)]
ACROSS = [(i, (i + 2) % RING) for i in range(RING)]


def expert_kernel(piece_rows, block, mb, rows_cap, width, ids, *refs):
    n_piece = len(piece_rows)
    pieces, refs = refs[:n_piece], refs[n_piece:]
    weights, refs = refs[:6], refs[6:]
    n_out = sum(piece_rows) // OUT
    outs, refs = refs[:n_out], refs[n_out:]
    sel_s, hid_s, wg_s, wu_s, wd_s, w_sem = refs
    w_copies = [
        pltpu.make_async_copy(weights[3 + j], dst, w_sem.at[j])
        for j, dst in enumerate((wg_s, wu_s, wd_s))
    ]
    for c in w_copies:
        c.start()
    total = sum(piece_rows)
    n_block = total // block
    hid = weights[0].shape[2]
    cut = []
    for i in range(n_piece):
        if cut and sum(piece_rows[j] for j in cut[-1]) < block:
            cut[-1].append(i)
        else:
            cut.append([i])

    def load(b, lo, hi):
        parts = [pieces[i][:, lo:hi] for i in cut[b]]
        return parts[0] if len(parts) == 1 else jnp.concatenate(parts, axis=0)

    def save(b, lo, hi, value):
        for i in range(block // OUT):
            outs[b * (block // OUT) + i][:, lo:hi] = value[i * OUT : (i + 1) * OUT]

    sel_s[...] = jnp.zeros(sel_s.shape, BF)

    def pick(shape, expert_axis):
        col = lax.broadcasted_iota(jnp.int32, shape, 1 - expert_axis)
        which = lax.broadcasted_iota(jnp.int32, shape, expert_axis)
        mine = jnp.where(which == 0, ids[0], ids[1])
        high = jnp.where(col == mine, 4.0, 0.0)
        low = jnp.where(col == mine + 32, 1.0, 0.0)
        return jnp.where(which < 2, high + low, 0.0).astype(BF)

    pick_row = pick((8, META), 0)
    pick_col = pick((META, META), 1)
    lane = lax.broadcasted_iota(jnp.int32, (block, block), 1)
    sub = lax.broadcasted_iota(jnp.int32, (block, block), 0)
    upper = jnp.where(sub <= lane, 1.0, 0.0).astype(BF)
    lower = jnp.where(lane <= sub, 1.0, 0.0).astype(BF)
    slot_row = lax.broadcasted_iota(jnp.int32, (WIN, block), 0)
    slot_col = lax.broadcasted_iota(jnp.int32, (block, WIN), 1)

    base = [jnp.int32(0), jnp.int32(0)]
    first, skew, wins, places = [], [], [], []
    for b in range(n_block):
        meta = load(b, width, width + META)
        num = lax.dot_general(pick_row, meta, (((1,), (1,)), ((), ())), preferred_element_type=F32)
        hit = jnp.where(num > 0.0, 1.0, 0.0)
        rank = jnp.dot(hit.astype(BF), upper, preferred_element_type=F32)
        places.append(jnp.where(num > 0.0, rank - 1.0, -1.0e4).astype(jnp.int32))
        start, off, need = [], [], []
        for e in range(2):
            count = jnp.sum(hit[e : e + 1, :]).astype(jnp.int32)
            s = pl.multiple_of((base[e] // 16) * 16, 16)
            start.append(s)
            off.append(base[e] - s)
            need.append(off[e] + count)
            base[e] = base[e] + count
        first.append(start)
        skew.append(off)
        wins.append(jnp.maximum(1, (jnp.maximum(need[0], need[1]) + WIN - 1) // WIN))
    single = functools.reduce(jnp.maximum, wins) == 1

    def select(b, k):
        chosen = [
            jnp.where(places[b][e : e + 1, :] + (skew[b][e] - k * WIN) == slot_row, 1.0, 0.0)
            for e in range(2)
        ]
        chosen = jnp.concatenate(chosen, axis=0).astype(BF)
        for lo in range(0, width + META, 512):
            hi = min(lo + 512, width + META)
            got = jnp.dot(chosen, load(b, lo, hi), preferred_element_type=F32).astype(BF)
            for e in range(2):
                to = pl.ds(pl.multiple_of(first[b][e] + k * WIN, 16), WIN)
                sel_s[e, to, lo:hi] = sel_s[e, to, lo:hi] + got[e * WIN : (e + 1) * WIN]

    @pl.when(single)
    def _():
        for b in range(n_block):
            select(b, 0)

    @pl.when(jnp.logical_not(single))
    def _():
        for b in range(n_block):

            def one(k, carry, b=b):
                select(b, k)
                return carry

            lax.fori_loop(0, wins[b], one, 0)

    for e in range(2):
        if e == 0:
            wg, wu, wd = weights[:3]
        else:
            wg, wu, wd = wg_s, wu_s, wd_s
            for c in w_copies:
                c.wait()

        def rows_of(m, carry, e=e, wg=wg, wu=wu, wd=wd):
            rows = pl.ds(pl.multiple_of(m * mb, mb), mb)

            for lo in range(0, hid, UP):
                x = sel_s[e, rows, :width]
                g = jnp.dot(x, wg[0, :, lo : lo + UP], preferred_element_type=F32)
                u = jnp.dot(x, wu[0, :, lo : lo + UP], preferred_element_type=F32)
                hid_s[:, lo : lo + UP] = (g / (1.0 + jnp.exp(-g)) * u).astype(BF)
            num = jnp.dot(sel_s[e, rows, width:], pick_col, preferred_element_type=F32)
            gate = num[:, e : e + 1] * (1.0 / GATE_DEN)

            for lo in range(0, width, DOWN):
                y = jnp.dot(hid_s[...], wd[0, :, lo : lo + DOWN], preferred_element_type=F32)
                sel_s[e, rows, lo : lo + DOWN] = (y * gate).astype(BF)
            return carry

        lax.fori_loop(0, (base[e] + mb - 1) // mb, rows_of, 0)

    columns = []
    for b in range(n_block):
        num = jnp.dot(load(b, width, width + META), pick_col, preferred_element_type=F32)
        hit = jnp.where(num > 0.0, 1.0, 0.0)
        rank = jnp.dot(lower, hit.astype(BF), preferred_element_type=F32)
        columns.append(jnp.where(num > 0.0, rank - 1.0, -1.0e4).astype(jnp.int32))

    def spread(b, k):
        hot = [
            jnp.where(columns[b][:, e : e + 1] + (skew[b][e] - k * WIN) == slot_col, 1.0, 0.0)
            for e in range(2)
        ]
        return jnp.concatenate(hot, axis=1).astype(BF)

    def put(b, k, lo, hot):
        y = jnp.concatenate(
            [
                sel_s[e, pl.ds(pl.multiple_of(first[b][e] + k * WIN, 16), WIN), lo : lo + STEP]
                for e in range(2)
            ],
            axis=0,
        )
        return jnp.dot(hot, y, preferred_element_type=F32)

    @pl.when(single)
    def _():
        for b in range(n_block):
            hot = spread(b, 0)
            for lo in range(0, width, STEP):
                save(b, lo, lo + STEP, put(b, 0, lo, hot).astype(BF))

    @pl.when(jnp.logical_not(single))
    def _():
        for b in range(n_block):
            for lo in range(0, width, STEP):

                def more(k, total, b=b, lo=lo):
                    return total + put(b, k, lo, spread(b, k))

                part = lax.fori_loop(0, wins[b], more, jnp.zeros((block, STEP), F32))
                save(b, lo, lo + STEP, part.astype(BF))


def in_vmem(x):
    return pltpu.with_memory_space_constraint(x, pltpu.VMEM)


def apply_experts(ids, pieces, weights):
    piece_rows = tuple(p.shape[0] for p in pieces)
    total = sum(piece_rows)
    width = pieces[0].shape[1] - META
    hid = weights[0].shape[2]
    block = 256
    most = 40 * (total // 64)
    mb = 192
    rows_cap = most + 2 * WIN
    n, n_out = len(pieces), total // OUT
    slots = 2 * most
    return pl.pallas_call(
        functools.partial(expert_kernel, piece_rows, block, mb, rows_cap, width),
        out_shape=[jax.ShapeDtypeStruct((OUT, width), BF)] * n_out,
        in_specs=[pl.BlockSpec(memory_space=pltpu.SMEM)]
        + [pl.BlockSpec(memory_space=pltpu.VMEM)] * (n + 3)
        + [pl.BlockSpec(memory_space=pltpu.HBM)] * 3,
        out_specs=[pl.BlockSpec(memory_space=pltpu.VMEM)] * n_out,
        scratch_shapes=[
            pltpu.VMEM((2, rows_cap, width + META), BF),
            pltpu.VMEM((mb, hid), BF),
            pltpu.VMEM((1, width, hid), BF),
            pltpu.VMEM((1, width, hid), BF),
            pltpu.VMEM((1, hid, width), BF),
            pltpu.SemaphoreType.DMA((3,)),
        ],
        compiler_params=pltpu.CompilerParams(vmem_limit_bytes=VMEM_LIMIT),
        cost_estimate=pl.CostEstimate(flops=slots * COST, bytes_accessed=0, transcendentals=0),
    )(ids, *[in_vmem(p) for p in pieces], *weights)


def add(*xs):
    total = xs[0].astype(F32)
    for x in xs[1:]:
        total = total + x.astype(F32)
    return total.astype(BF)


def to_next(x, axis):
    return lax.ppermute(x, axis, NEXT)


def to_prev(x, axis):
    return lax.ppermute(x, axis, PREV)


def near(streams):
    return [(to_next(x, axis), to_prev(x, axis)) for x, axis in streams]


def after(x, *first):
    return lax.optimization_barrier((x, first))[0]


def body(tokens, routes, gate_num, w_gate, w_up, w_down):
    half = tokens.shape[0] // 2
    own = lax.axis_index(("x", "y", "core"))
    ids = jnp.stack([own, own ^ 1]).astype(jnp.int32)
    swap = [(0, 1), (1, 0)]

    experts = jnp.arange(32, dtype=jnp.int32)
    num = jnp.sum(jnp.where(routes[:, :, None] == experts, gate_num[:, :, None], 0), axis=1)
    meta = jnp.concatenate(
        [num >> 2, num & 3, jnp.zeros((tokens.shape[0], META - 64), jnp.int32)], axis=1
    )
    rows = jnp.concatenate([tokens, meta.astype(BF)], axis=1)

    streams = [(rows[:half], "x"), (rows[half:], "y")]
    p_gate = lax.ppermute(w_gate, "core", swap)
    p_up = lax.ppermute(w_up, "core", swap)
    (xa, ax), (ya, ay) = streams
    y_prev = to_next(ya, ay)
    x_prev = to_next(xa, ax)
    x_next = to_prev(xa, ax)
    y_next = to_prev(after(ya, y_prev), ay)
    x_far = lax.ppermute(after(xa, x_prev), ax, ACROSS)
    y_far = lax.ppermute(after(ya, x_next, x_prev), ay, ACROSS)
    halves = [
        (jnp.concatenate([xa, x_prev]), jnp.concatenate([x_next, x_far])),
        (jnp.concatenate([ya, y_prev]), jnp.concatenate([y_next, y_far])),
    ]
    halves, p_gate, p_up, w_down_late = lax.optimization_barrier((halves, p_gate, p_up, w_down))
    p_down = lax.ppermute(w_down_late, "core", swap)
    weights = [in_vmem(w) for w in (w_gate, w_up, w_down)] + [p_gate, p_up, p_down]
    axes = ["y", "x"]
    one = [(to_next(h0, ax), to_prev(h1, ax)) for (h0, h1), ax in zip(halves, axes)]
    two = []
    for (a, b), (h0, h1), ax in zip(one, halves, axes):
        two.append((to_next(after(h1, a), ax), to_prev(after(h0, b), ax)))
    early = apply_experts(ids, [*one[0], *one[1]], weights)
    opp = []
    for (a, b), (c, d), ax in zip(one, two, axes):
        opp.append((to_next(after(a, c, early), ax), to_prev(after(b, d, early), ax)))
    here = apply_experts(ids, after([*halves[0], *halves[1]], two, early), weights)
    gone = []
    for i, ((a, b), ax) in enumerate(zip(opp, axes)):
        gone.append(
            (to_next(after(early[2 * i + 1], a, here), ax), to_prev(after(early[2 * i], b, here), ax))
        )
    across = apply_experts(ids, [*opp[0], *opp[1]], weights)
    late = apply_experts(ids, after([*two[0], *two[1]], gone, across), weights)
    passed = []
    for i, ((a, b), ax) in enumerate(zip(gone, axes)):
        passed.append(
            (to_next(after(across[2 * i], a), ax), to_prev(after(across[2 * i + 1], b), ax))
        )
    firsts = []
    for i, ((a, b), (f, g), ax) in enumerate(zip(gone, passed, axes)):
        c = to_next(add(late[2 * i + 1], f), ax)
        d = to_prev(add(late[2 * i], g), ax)
        firsts.append((add(here[2 * i], c, b), add(here[2 * i + 1], a, d)))
    sums = []
    for (h0, h1), axis in zip(firsts, ["x", "y"]):
        sums.append(
            add(
                h0[:half],
                to_prev(h0[half:], axis),
                to_next(h1[:half], axis),
                lax.ppermute(h1[half:], axis, ACROSS),
            )
        )
    return jnp.concatenate(sums)


def solution(mesh):
    fine = Mesh(
        mesh.devices.reshape(mesh.shape["dp"], RING, RING, 2), ("dp", "x", "y", "core")
    )
    rows = P(("dp", "x", "y", "core"), None)
    expert = P(("x", "y", "core"), None, None)
    return jax.shard_map(
        body,
        mesh=fine,
        in_specs=(rows, rows, rows, expert, expert, expert),
        out_specs=rows,
        check_vma=False,
    )
```

```python
import functools

import jax
import jax.numpy as jnp
from jax import lax
from jax.experimental import pallas as pl
from jax.experimental.pallas import tpu as pltpu
from jax.sharding import Mesh, PartitionSpec as P

GATE_DEN = 1024
META = 128
WIN = 128
OUT = 128
STEP = 512
COST = 1000
UP = 256
DOWN = 512
VMEM_LIMIT = 26 * 1024 * 1024
BF = jnp.bfloat16
F32 = jnp.float32
RING = 4
NEXT = [(i, (i + 1) % RING) for i in range(RING)]
PREV = [(i, (i + RING - 1) % RING) for i in range(RING)]
ACROSS = [(i, (i + 2) % RING) for i in range(RING)]


def expert_kernel(piece_rows, block, mb, rows_cap, width, ids, *refs):
    n_piece = len(piece_rows)
    pieces, refs = refs[:n_piece], refs[n_piece:]
    weights, refs = refs[:6], refs[6:]
    n_out = sum(piece_rows) // OUT
    outs, refs = refs[:n_out], refs[n_out:]
    sel_s, hid_s, wg_s, wu_s, wd_s, w_sem = refs
    w_copies = [
        pltpu.make_async_copy(weights[3 + j], dst, w_sem.at[j])
        for j, dst in enumerate((wg_s, wu_s, wd_s))
    ]
    for c in w_copies:
        c.start()
    total = sum(piece_rows)
    n_block = total // block
    hid = weights[0].shape[2]
    cut = []
    for i in range(n_piece):
        if cut and sum(piece_rows[j] for j in cut[-1]) < block:
            cut[-1].append(i)
        else:
            cut.append([i])

    def load(b, lo, hi):
        parts = [pieces[i][:, lo:hi] for i in cut[b]]
        return parts[0] if len(parts) == 1 else jnp.concatenate(parts, axis=0)

    def save(b, lo, hi, value):
        for i in range(block // OUT):
            outs[b * (block // OUT) + i][:, lo:hi] = value[i * OUT : (i + 1) * OUT]

    sel_s[...] = jnp.zeros(sel_s.shape, BF)

    def pick(shape, expert_axis):
        col = lax.broadcasted_iota(jnp.int32, shape, 1 - expert_axis)
        which = lax.broadcasted_iota(jnp.int32, shape, expert_axis)
        mine = jnp.where(which == 0, ids[0], ids[1])
        high = jnp.where(col == mine, 4.0, 0.0)
        low = jnp.where(col == mine + 32, 1.0, 0.0)
        return jnp.where(which < 2, high + low, 0.0).astype(BF)

    pick_row = pick((8, META), 0)
    pick_col = pick((META, META), 1)
    lane = lax.broadcasted_iota(jnp.int32, (block, block), 1)
    sub = lax.broadcasted_iota(jnp.int32, (block, block), 0)
    upper = jnp.where(sub <= lane, 1.0, 0.0).astype(BF)
    lower = jnp.where(lane <= sub, 1.0, 0.0).astype(BF)
    slot_row = lax.broadcasted_iota(jnp.int32, (WIN, block), 0)
    slot_col = lax.broadcasted_iota(jnp.int32, (block, WIN), 1)

    base = [jnp.int32(0), jnp.int32(0)]
    first, skew, wins, places = [], [], [], []
    for b in range(n_block):
        meta = load(b, width, width + META)
        num = lax.dot_general(pick_row, meta, (((1,), (1,)), ((), ())), preferred_element_type=F32)
        hit = jnp.where(num > 0.0, 1.0, 0.0)
        rank = jnp.dot(hit.astype(BF), upper, preferred_element_type=F32)
        places.append(jnp.where(num > 0.0, rank - 1.0, -1.0e4).astype(jnp.int32))
        start, off, need = [], [], []
        for e in range(2):
            count = jnp.sum(hit[e : e + 1, :]).astype(jnp.int32)
            s = pl.multiple_of((base[e] // 16) * 16, 16)
            start.append(s)
            off.append(base[e] - s)
            need.append(off[e] + count)
            base[e] = base[e] + count
        first.append(start)
        skew.append(off)
        wins.append(jnp.maximum(1, (jnp.maximum(need[0], need[1]) + WIN - 1) // WIN))
    single = functools.reduce(jnp.maximum, wins) == 1

    def select(b, k):
        chosen = [
            jnp.where(places[b][e : e + 1, :] + (skew[b][e] - k * WIN) == slot_row, 1.0, 0.0)
            for e in range(2)
        ]
        chosen = jnp.concatenate(chosen, axis=0).astype(BF)
        for lo in range(0, width + META, 512):
            hi = min(lo + 512, width + META)
            got = jnp.dot(chosen, load(b, lo, hi), preferred_element_type=F32).astype(BF)
            for e in range(2):
                to = pl.ds(pl.multiple_of(first[b][e] + k * WIN, 16), WIN)
                sel_s[e, to, lo:hi] = sel_s[e, to, lo:hi] + got[e * WIN : (e + 1) * WIN]

    @pl.when(single)
    def _():
        for b in range(n_block):
            select(b, 0)

    @pl.when(jnp.logical_not(single))
    def _():
        for b in range(n_block):

            def one(k, carry, b=b):
                select(b, k)
                return carry

            lax.fori_loop(0, wins[b], one, 0)

    for e in range(2):
        if e == 0:
            wg, wu, wd = weights[:3]
        else:
            wg, wu, wd = wg_s, wu_s, wd_s
            for c in w_copies:
                c.wait()

        def rows_of(m, carry, e=e, wg=wg, wu=wu, wd=wd):
            rows = pl.ds(pl.multiple_of(m * mb, mb), mb)

            for lo in range(0, hid, UP):
                x = sel_s[e, rows, :width]
                g = jnp.dot(x, wg[0, :, lo : lo + UP], preferred_element_type=F32)
                u = jnp.dot(x, wu[0, :, lo : lo + UP], preferred_element_type=F32)
                hid_s[:, lo : lo + UP] = (g / (1.0 + jnp.exp(-g)) * u).astype(BF)
            num = jnp.dot(sel_s[e, rows, width:], pick_col, preferred_element_type=F32)
            gate = num[:, e : e + 1] * (1.0 / GATE_DEN)

            for lo in range(0, width, DOWN):
                y = jnp.dot(hid_s[...], wd[0, :, lo : lo + DOWN], preferred_element_type=F32)
                sel_s[e, rows, lo : lo + DOWN] = (y * gate).astype(BF)
            return carry

        lax.fori_loop(0, (base[e] + mb - 1) // mb, rows_of, 0)

    columns = []
    for b in range(n_block):
        num = jnp.dot(load(b, width, width + META), pick_col, preferred_element_type=F32)
        hit = jnp.where(num > 0.0, 1.0, 0.0)
        rank = jnp.dot(lower, hit.astype(BF), preferred_element_type=F32)
        columns.append(jnp.where(num > 0.0, rank - 1.0, -1.0e4).astype(jnp.int32))

    def spread(b, k):
        hot = [
            jnp.where(columns[b][:, e : e + 1] + (skew[b][e] - k * WIN) == slot_col, 1.0, 0.0)
            for e in range(2)
        ]
        return jnp.concatenate(hot, axis=1).astype(BF)

    def put(b, k, lo, hot):
        y = jnp.concatenate(
            [
                sel_s[e, pl.ds(pl.multiple_of(first[b][e] + k * WIN, 16), WIN), lo : lo + STEP]
                for e in range(2)
            ],
            axis=0,
        )
        return jnp.dot(hot, y, preferred_element_type=F32)

    @pl.when(single)
    def _():
        for b in range(n_block):
            hot = spread(b, 0)
            for lo in range(0, width, STEP):
                save(b, lo, lo + STEP, put(b, 0, lo, hot).astype(BF))

    @pl.when(jnp.logical_not(single))
    def _():
        for b in range(n_block):
            for lo in range(0, width, STEP):

                def more(k, total, b=b, lo=lo):
                    return total + put(b, k, lo, spread(b, k))

                part = lax.fori_loop(0, wins[b], more, jnp.zeros((block, STEP), F32))
                save(b, lo, lo + STEP, part.astype(BF))


def in_vmem(x):
    return pltpu.with_memory_space_constraint(x, pltpu.VMEM)


def apply_experts(ids, pieces, weights):
    piece_rows = tuple(p.shape[0] for p in pieces)
    total = sum(piece_rows)
    width = pieces[0].shape[1] - META
    hid = weights[0].shape[2]
    block = 256
    most = 40 * (total // 64)
    mb = 192
    rows_cap = most + 2 * WIN
    n, n_out = len(pieces), total // OUT
    slots = 2 * most
    return pl.pallas_call(
        functools.partial(expert_kernel, piece_rows, block, mb, rows_cap, width),
        out_shape=[jax.ShapeDtypeStruct((OUT, width), BF)] * n_out,
        in_specs=[pl.BlockSpec(memory_space=pltpu.SMEM)]
        + [pl.BlockSpec(memory_space=pltpu.VMEM)] * (n + 3)
        + [pl.BlockSpec(memory_space=pltpu.HBM)] * 3,
        out_specs=[pl.BlockSpec(memory_space=pltpu.VMEM)] * n_out,
        scratch_shapes=[
            pltpu.VMEM((2, rows_cap, width + META), BF),
            pltpu.VMEM((mb, hid), BF),
            pltpu.VMEM((1, width, hid), BF),
            pltpu.VMEM((1, width, hid), BF),
            pltpu.VMEM((1, hid, width), BF),
            pltpu.SemaphoreType.DMA((3,)),
        ],
        compiler_params=pltpu.CompilerParams(vmem_limit_bytes=VMEM_LIMIT),
        cost_estimate=pl.CostEstimate(flops=slots * COST, bytes_accessed=0, transcendentals=0),
    )(ids, *[in_vmem(p) for p in pieces], *weights)


def add(*xs):
    total = xs[0].astype(F32)
    for x in xs[1:]:
        total = total + x.astype(F32)
    return total.astype(BF)


def to_next(x, axis):
    return lax.ppermute(x, axis, NEXT)


def to_prev(x, axis):
    return lax.ppermute(x, axis, PREV)


def near(streams):
    return [(to_next(x, axis), to_prev(x, axis)) for x, axis in streams]


def after(x, *first):
    return lax.optimization_barrier((x, first))[0]


def body(tokens, routes, gate_num, w_gate, w_up, w_down):
    half = tokens.shape[0] // 2
    own = lax.axis_index(("x", "y", "core"))
    ids = jnp.stack([own, own ^ 1]).astype(jnp.int32)
    swap = [(0, 1), (1, 0)]

    experts = jnp.arange(32, dtype=jnp.int32)
    num = jnp.sum(jnp.where(routes[:, :, None] == experts, gate_num[:, :, None], 0), axis=1)
    meta = jnp.concatenate(
        [num >> 2, num & 3, jnp.zeros((tokens.shape[0], META - 64), jnp.int32)], axis=1
    )
    rows = jnp.concatenate([tokens, meta.astype(BF)], axis=1)

    streams = [(rows[:half], "x"), (rows[half:], "y")]
    p_gate = lax.ppermute(w_gate, "core", swap)
    p_up = lax.ppermute(w_up, "core", swap)
    (xa, ax), (ya, ay) = streams
    y_prev = to_next(ya, ay)
    x_prev = to_next(xa, ax)
    x_next = to_prev(xa, ax)
    y_next = to_prev(after(ya, y_prev), ay)
    x_far = lax.ppermute(after(xa, x_prev), ax, ACROSS)
    y_far = lax.ppermute(after(ya, x_next, x_prev), ay, ACROSS)
    halves = [
        (jnp.concatenate([xa, x_prev]), jnp.concatenate([x_next, x_far])),
        (jnp.concatenate([ya, y_prev]), jnp.concatenate([y_next, y_far])),
    ]
    halves, p_gate, p_up, w_down_late = lax.optimization_barrier((halves, p_gate, p_up, w_down))
    p_down = lax.ppermute(w_down_late, "core", swap)
    weights = [in_vmem(w) for w in (w_gate, w_up, w_down)] + [p_gate, p_up, p_down]
    axes = ["y", "x"]
    one = [(to_next(h0, ax), to_prev(h1, ax)) for (h0, h1), ax in zip(halves, axes)]
    here = apply_experts(ids, [*halves[0], *halves[1]], weights)
    two = []
    for (a, b), (h0, h1), ax in zip(one, halves, axes):
        two.append((to_next(after(h1, a, here), ax), to_prev(after(h0, b, here), ax)))
    early = apply_experts(ids, [*one[0], *one[1]], weights)
    opp = []
    for (a, b), (c, d), ax in zip(one, two, axes):
        opp.append((to_next(after(a, c, early), ax), to_prev(after(b, d, early), ax)))
    gone = []
    for i, ((a, b), ax) in enumerate(zip(opp, axes)):
        gone.append(
            (to_next(after(early[2 * i + 1], a), ax), to_prev(after(early[2 * i], b), ax))
        )
    across = apply_experts(ids, [*opp[0], *opp[1]], weights)
    late = apply_experts(ids, after([*two[0], *two[1]], gone, across), weights)
    passed = []
    for i, ((a, b), ax) in enumerate(zip(gone, axes)):
        passed.append(
            (to_next(after(across[2 * i], a), ax), to_prev(after(across[2 * i + 1], b), ax))
        )
    firsts = []
    for i, ((a, b), (f, g), ax) in enumerate(zip(gone, passed, axes)):
        c = to_next(add(late[2 * i + 1], f), ax)
        d = to_prev(add(late[2 * i], g), ax)
        firsts.append((add(here[2 * i], c, b), add(here[2 * i + 1], a, d)))
    sums = []
    for (h0, h1), axis in zip(firsts, ["x", "y"]):
        sums.append(
            add(
                h0[:half],
                to_prev(h0[half:], axis),
                to_next(h1[:half], axis),
                lax.ppermute(h1[half:], axis, ACROSS),
            )
        )
    return jnp.concatenate(sums)


def solution(mesh):
    fine = Mesh(
        mesh.devices.reshape(mesh.shape["dp"], RING, RING, 2), ("dp", "x", "y", "core")
    )
    rows = P(("dp", "x", "y", "core"), None)
    expert = P(("x", "y", "core"), None, None)
    return jax.shard_map(
        body,
        mesh=fine,
        in_specs=(rows, rows, rows, expert, expert, expert),
        out_specs=rows,
        check_vma=False,
    )
```
